32 devices in a mesh: mat: 8 (over y, x, core), frac: 4 (over z).
Axes of the slice: x: 2, y: 2, z: 4, core: 2. Of those that a mesh axis runs over, the one named last changes fastest.
Arguments:
- pressure: float32 [256, 128, 256], P('mat', 'frac'), may hold values from -6 to 6
- source: float32 [256, 128, 256], P('mat', 'frac'), may hold values from -12 to 12
- storage: float32 [256, 128, 256], P('mat', 'frac'), may hold values from 0.25 to 2
- matrix_conc: float32 [256, 128, 256], P('mat', 'frac'), may hold values from -6 to 6
- frac_pressure: float32 [512, 128], P(('mat', 'frac')), may hold values from -6 to 6
- frac_conc: float32 [512, 128], P(('mat', 'frac')), may hold values from -6 to 6
- tile_blocks: bfloat16 [512, 8, 128, 128], P(('mat', 'frac')), may hold values from -0.5 to 0.5
- tile_links: int32 [512, 8], P(('mat', 'frac')), may hold values from 0 to 63
- tile_dir: int32 [512, 8], P(('mat', 'frac')), may hold values from 0 to 1
- link_cell: int32 [1024, 64], P(('mat', 'frac')), may hold values from 0 to 262143
- link_frac: int32 [1024, 64], P(('mat', 'frac')), may hold values from 0 to 2047
- link_trans: float32 [1024, 64], P(('mat', 'frac')), may hold values from 0.05 to 1
- link_count: int32 [1024], P(('mat', 'frac')), may hold values from 1 to 64
Outputs:
- smoothed: float32 [256, 128, 256], P('mat', 'frac')
- matrix_out: float32 [256, 128, 256], P('mat', 'frac')
- frac_out: float32 [512, 128], P(('mat', 'frac'))
The draws below stay inside these ranges and needn't reach their ends.
Inputs may be any that keep to these rules, and one draw needn't show every extreme that they name: `tile_links`: indices among the 64 tiles of the devices that share the mat index.
All inputs are finite; a program needn't handle non-finite values.
Results may differ from the reference program's by a relative error of at most 0.00056.
Values may be sent and summed in bfloat16 or wider, within the bound.
A program may use at most 128 MiB of HBM per device.

```python
import math
import jax
import jax.numpy as jnp
from jax import lax

CX = 32
CY = 32
CZ = 256
TILE = 128
TILE_DEV = 16
K = 8
CAP = 64
SWEEPS = 2
NX = 256
NY = 128
TILES = 512
N_MAT = 8
N_FRAC = 4
DEVICES = 32


def draw_link_count(key, part):
    key_load, key_spread, key_full = jax.random.split(key, 3)
    devices = N_MAT * N_FRAC
    load_factor = jax.random.randint(key_load, (devices,), 1, 5)
    weights = jnp.tile(load_factor, devices)
    spread = jax.random.randint(key_spread, (devices * devices,), 0, CAP)
    counts = jnp.minimum(CAP, jnp.maximum(1, CAP // 4 + spread * weights // 2))
    chosen = jax.random.randint(key_full, (), 0, devices * devices)
    return counts.at[chosen].set(CAP).astype(jnp.int32)


def set_ends(array, rng, low, largest):
    spot = [jax.random.randint(jax.random.fold_in(rng, axis), (), 0, length) for axis, length in enumerate(array.shape)]
    main_axis = array.shape.index(max(array.shape))
    next_to = spot[:main_axis] + [(spot[main_axis] + 1) % array.shape[main_axis]] + spot[main_axis + 1:]
    return array.at[tuple(spot)].set(low).at[tuple(next_to)].set(largest)


def steps_of(rng, shape, shards, low, top_value):
    def one(axis_at, parts):
        heights = jax.random.uniform(jax.random.fold_in(jax.random.fold_in(rng, 6), axis_at), (parts,), jnp.float32, low / len(shards), top_value / len(shards))
        return jnp.repeat(jnp.exp(heights), shape[axis_at] // parts).reshape((-1,) + (1,) * (len(shape) - axis_at - 1))

    gain = one(*shards[0])
    for cut in shards[1:]:
        gain = gain * one(*cut)
    return gain


def gaussian(key, dims, width, most, cuts=(), held_as=jnp.bfloat16):
    values = width * jax.random.normal(key, dims, jnp.float32)
    if cuts:
        values = values * steps_of(key, dims, cuts, -0.22, 0.18)
    return jnp.clip(values, -most, most).astype(held_as)


def setup_inputs(seed: int = 0) -> dict:
    key_list = jax.random.split(jax.random.key(seed), 14)
    pressure = gaussian(key_list[0], (NX, NY, CZ), 1.0, 6.0, ((0, 8), (1, 4)), jnp.float32)
    source = gaussian(key_list[1], (NX, NY, CZ), 2.0, 12.0, ((0, 8), (1, 4)), jnp.float32)
    storage = jnp.clip(0.25 + 1.75 * jax.random.uniform(key_list[2], (NX, NY, CZ), jnp.float32) ** steps_of(key_list[2], (NX, NY, CZ), ((0, 8), (1, 4)), -0.2, 0.2), 0.25, 2.0)
    matrix_conc = gaussian(key_list[3], (NX, NY, CZ), 1.0, 6.0, ((0, 8), (1, 4)), jnp.float32)
    frac_pressure = gaussian(key_list[4], (TILES, TILE), 1.0, 6.0, ((0, 32),), jnp.float32)
    frac_conc = gaussian(key_list[5], (TILES, TILE), 1.0, 6.0, ((0, 32),), jnp.float32)
    tile_blocks = gaussian(key_list[6], (TILES, K, TILE, TILE), TILE ** -0.5, 0.5, ((0, 32),))
    tile_links = set_ends(jax.random.randint(key_list[7], (TILES, K), 0, TILE_DEV * N_FRAC), jax.random.fold_in(key_list[7], 1), 0, (TILE_DEV * N_FRAC) - 1).astype(jnp.int32)
    tile_dir = set_ends(jax.random.randint(key_list[8], (TILES, K), 0, 2), jax.random.fold_in(key_list[8], 1), 0, 1).astype(jnp.int32)
    link_cell = set_ends(jax.random.randint(key_list[9], (DEVICES * DEVICES, CAP), 0, CX * CY * CZ), jax.random.fold_in(key_list[9], 1), 0, (CX * CY * CZ) - 1).astype(jnp.int32)
    link_frac = set_ends(jax.random.randint(key_list[10], (DEVICES * DEVICES, CAP), 0, TILE_DEV * TILE), jax.random.fold_in(key_list[10], 1), 0, (TILE_DEV * TILE) - 1).astype(jnp.int32)
    link_trans = jnp.clip(jnp.exp(math.log(1.0) - 2.9957323 * jax.random.uniform(key_list[11], (DEVICES * DEVICES, CAP), jnp.float32) ** steps_of(key_list[11], (DEVICES * DEVICES, CAP), ((0, 32),), -0.2, 0.2)), 0.05, 1.0)
    link_count = draw_link_count(jax.random.fold_in(key_list[13], 71), 0)
    return dict(pressure=pressure, source=source, storage=storage, matrix_conc=matrix_conc, frac_pressure=frac_pressure, frac_conc=frac_conc, tile_blocks=tile_blocks, tile_links=tile_links, tile_dir=tile_dir, link_cell=link_cell, link_frac=link_frac, link_trans=link_trans, link_count=link_count)


OMEGA = 0.8
DT_FRAC = 0.1
DT_MATRIX = 0.5


def sweep(field, storage, source):
    padded = jnp.pad(field, 1)
    beside = padded[2:, 1:-1, 1:-1] + padded[:-2, 1:-1, 1:-1]
    beside = beside + padded[1:-1, 2:, 1:-1] + padded[1:-1, :-2, 1:-1]
    beside = beside + padded[1:-1, 1:-1, 2:] + padded[1:-1, 1:-1, :-2]
    diagonal = 6.0 + storage
    return field + OMEGA * (source - (diagonal * field - beside)) / diagonal


def blocks_of(field):
    shaped = field.reshape(N_MAT, CX, N_FRAC, CY, CZ).transpose(0, 2, 1, 3, 4)
    return shaped.reshape(N_MAT * N_FRAC, CX * CY * CZ)


def grid_of(blocks):
    shaped = blocks.reshape(N_MAT, N_FRAC, CX, CY, CZ).transpose(0, 2, 1, 3, 4)
    return shaped.reshape(N_MAT * CX, N_FRAC * CY, CZ)


def tile_step(inputs):
    blocks, picked, dirs, conc, transfer = inputs
    widened = blocks.astype(jnp.float32)
    chosen = jnp.where(dirs[..., None] == 1, picked.astype(jnp.float32), 0.0)
    inflow = jnp.einsum("tkij,tkj->ti", widened, chosen)
    row_sums = jnp.sum(widened, axis=3)
    outflow = jnp.sum(jnp.where(dirs[..., None] == 0, row_sums, 0.0), axis=1) * conc
    return conc + DT_FRAC * (inflow - outflow + transfer)


def reference(pressure, source, storage, matrix_conc, frac_pressure, frac_conc, tile_blocks, tile_links, tile_dir, link_cell, link_frac, link_trans, link_count):
    devices = N_MAT * N_FRAC
    cells_dev = CX * CY * CZ
    frac_dev = TILE_DEV * TILE
    smoothed = pressure
    for repeat in range(SWEEPS):
        smoothed = sweep(smoothed, storage, source)
    field_blocks = blocks_of(smoothed)
    conc_blocks = blocks_of(matrix_conc)
    row_ids = jnp.arange(devices * devices, dtype=jnp.int32)
    sender = row_ids // devices
    owner_ids = row_ids % devices
    live_mask = jnp.arange(CAP, dtype=jnp.int32)[None, :] < link_count[:, None]
    live_trans = jnp.where(live_mask, link_trans, 0.0)
    at_cells = field_blocks[sender[:, None], link_cell]
    frac_index = owner_ids[:, None] * frac_dev + link_frac
    total_fracs = devices * frac_dev
    first_sum = jax.ops.segment_sum((live_trans * at_cells).ravel(), frac_index.ravel(), total_fracs)
    second_sum = jax.ops.segment_sum(live_trans.ravel(), frac_index.ravel(), total_fracs)
    transfer = first_sum - frac_pressure.reshape(-1) * second_sum
    tile_conc = frac_conc.astype(jnp.bfloat16)
    group_size = TILE_DEV * N_FRAC
    tile_ids = jnp.arange(devices * TILE_DEV, dtype=jnp.int32)
    source_tiles = (tile_ids // group_size)[:, None] * group_size + tile_links
    picked = tile_conc[source_tiles]
    frac_out = lax.map(tile_step, (
        tile_blocks.reshape(devices, TILE_DEV, K, TILE, TILE),
        picked.reshape(devices, TILE_DEV, K, TILE),
        tile_dir.reshape(devices, TILE_DEV, K),
        frac_conc.reshape(devices, TILE_DEV, TILE),
        transfer.reshape(devices, TILE_DEV, TILE)))
    frac_out = frac_out.reshape(devices * TILE_DEV, TILE)
    returned = frac_out.reshape(-1)[frac_index]
    local_conc = conc_blocks[sender[:, None], link_cell]
    link_terms = live_trans * (returned - local_conc)
    cell_index = sender[:, None] * cells_dev + link_cell
    change = jax.ops.segment_sum(link_terms.ravel(), cell_index.ravel(), devices * cells_dev)
    matrix_out = conc_blocks + DT_MATRIX * change.reshape(devices, cells_dev)
    return smoothed, grid_of(matrix_out), frac_out
```

```python
import functools

import jax
import jax.numpy as jnp
from jax import lax
from jax.experimental import pallas as pl
from jax.experimental.pallas import tpu as pltpu
from jax.sharding import PartitionSpec as P

OMEGA = 0.8
DT_FRAC = 0.1
DT_MATRIX = 0.5
MESH = pl.DeviceIdType.MESH
F32 = jnp.float32
BF16 = jnp.bfloat16
LANES = 128
NT = (((1,), (1,)), ((), ()))


def split(v):
    high = v.astype(BF16)
    return high, (v - high.astype(F32)).astype(BF16)


def kernel(
    nm, nf,
    pressure, source, storage, conc, blocks, frac_pressure, frac_conc, tile_links, tile_dir, cell, pack,
    out_s, out_m, out_f,
    pv, sv, rv, cv, fv, bv, yst, hx, hy, hot, ft, place, lhs, wt,
    conc_at, field_at, rets, rx0, rx1, rx2, group, xin, xout, inflow, outflow,
    load_sem, store_sem, halo_send, halo_recv, a2a_send, a2a_recv, group_send, group_recv,
):
    m, f = lax.axis_index("mat"), lax.axis_index("frac")
    peers = nm * nf
    rows = peers // 2
    me = m * nf + f
    nx, ny, nz = pv.shape
    zbits = nz.bit_length() - 1
    tiles, tsize = frac_conc.shape
    tbits = tsize.bit_length() - 1
    kk = bv.shape[1]
    cells = nx * ny

    loads = [
        pltpu.make_async_copy(a, b, load_sem.at[i])
        for i, (a, b) in enumerate(
            ((pressure, pv), (storage, sv), (source, rv), (conc, cv), (blocks, bv))
        )
    ]
    for copy in loads:
        copy.start()

    barrier = pltpu.get_barrier_semaphore()

    def greet(i, carry):
        dest = lax.rem(me + i, peers)
        pl.semaphore_signal(
            barrier, inc=1, device_id=(lax.div(dest, nf), lax.rem(dest, nf)), device_id_type=MESH
        )
        return carry

    lax.fori_loop(1, peers, greet, 0)

    @pl.when(m == 0)
    def _():
        for k in range(2):
            hx[k, 0] = jnp.zeros((ny, nz), F32)

    @pl.when(m == nm - 1)
    def _():
        for k in range(2):
            hx[k, 1] = jnp.zeros((ny, nz), F32)

    @pl.when(f == 0)
    def _():
        for k in range(2):
            hy[k, 0] = jnp.zeros((nx, nz), F32)

    @pl.when(f == nf - 1)
    def _():
        for k in range(2):
            hy[k, 1] = jnp.zeros((nx, nz), F32)

    group[f] = frac_conc[...].astype(BF16)

    loads[0].wait()

    def stage(x, carry):
        yst[0, 0, pl.ds(x, 1), :] = pv[x, 0:1, :]
        yst[0, 1, pl.ds(x, 1), :] = pv[x, ny - 1 : ny, :]
        return carry

    lax.fori_loop(0, nx, stage, 0)

    def halo(k, field):
        out = []
        for d, (src, dst, to, sends, gets) in enumerate((
            (field.at[0], hx.at[k, 1], (m - 1, f), m > 0, m < nm - 1),
            (field.at[nx - 1], hx.at[k, 0], (m + 1, f), m < nm - 1, m > 0),
            (yst.at[k, 0], hy.at[k, 1], (m, f - 1), f > 0, f < nf - 1),
            (yst.at[k, 1], hy.at[k, 0], (m, f + 1), f < nf - 1, f > 0),
        )):
            copy = pltpu.make_async_remote_copy(
                src_ref=src, dst_ref=dst, send_sem=halo_send.at[k, d], recv_sem=halo_recv.at[k, d],
                device_id=to, device_id_type=MESH,
            )
            out.append((copy, sends, gets))
        return out

    def start_halo(copies):
        for copy, sends, gets in copies:
            pl.when(sends)(copy.start)

    def wait_halo(copies):
        for copy, sends, gets in copies:
            pl.when(gets)(copy.wait_recv)
        for copy, sends, gets in copies:
            pl.when(sends)(copy.wait_send)

    def exchange(src, dst, k):
        def send(i, carry):
            dest = lax.rem(me + i, peers)
            pltpu.make_async_remote_copy(
                src_ref=src.at[lax.rem(dest, rows)], dst_ref=dst.at[me],
                send_sem=a2a_send.at[k], recv_sem=a2a_recv.at[k],
                device_id=(lax.div(dest, nf), lax.rem(dest, nf)), device_id_type=MESH,
            ).start()
            return carry

        lax.fori_loop(1, peers, send, 0)
        dst[me] = src[lax.rem(me, rows)]

    def wait_exchange(dst, k):
        part = dst.at[pl.ds(0, peers - 1)]
        pltpu.make_async_copy(part, part, a2a_recv.at[k]).wait()
        pltpu.make_async_copy(part, part, a2a_send.at[k]).wait()

    pl.semaphore_wait(barrier, peers - 1)
    first = halo(0, pv)
    start_halo(first)
    exchange(pack, rx0, 0)

    def spread(i, carry):
        pltpu.make_async_remote_copy(
            src_ref=group.at[f], dst_ref=group.at[f], send_sem=group_send, recv_sem=group_recv,
            device_id=(m, lax.rem(f + i, nf)), device_id_type=MESH,
        ).start()
        return carry

    lax.fori_loop(1, nf, spread, 0)

    upper = me >= rows
    lane = lax.broadcasted_iota(jnp.int32, (1, LANES), 1)
    left = lane < LANES // 2

    def joined(a, b):
        a = jnp.where(upper, pltpu.roll(a, LANES // 2, 1), a)
        b = jnp.where(upper, b, pltpu.roll(b, LANES // 2, 1))
        return jnp.where(left, a, b)

    def at(r):
        return pl.ds(pl.multiple_of(r * LANES, LANES), LANES)

    row_ids = lax.broadcasted_iota(jnp.int32, (cells, LANES), 0)

    def mark(r, carry):
        high = lax.shift_right_logical(cell[r], zbits)
        hot[:, at(r)] = jnp.where(row_ids == high, 1.0, 0.0).astype(BF16)
        return carry

    lax.fori_loop(0, rows, mark, 0)

    loads[1].wait()
    loads[2].wait()

    def factors(x, carry):
        scale = OMEGA / (6.0 + sv[x])
        sv[x] = scale
        rv[x] = rv[x] * scale
        return carry

    lax.fori_loop(0, nx, factors, 0)

    iy = lax.broadcasted_iota(jnp.int32, (ny, nz), 0)
    iz = lax.broadcasted_iota(jnp.int32, (ny, nz), 1)

    def sweep(src, dst, k, faces):
        def slab(x, carry):
            cur = src[x]
            before = jnp.where(x == 0, hx[k, 0], src[jnp.maximum(x - 1, 0)])
            after = jnp.where(x == nx - 1, hx[k, 1], src[jnp.minimum(x + 1, nx - 1)])
            beside = before + after
            beside += jnp.where(iy == 0, hy[k, 0, pl.ds(x, 1), :], pltpu.roll(cur, 1, 0))
            beside += jnp.where(iy == ny - 1, hy[k, 1, pl.ds(x, 1), :], pltpu.roll(cur, ny - 1, 0))
            beside += jnp.where(iz == 0, 0.0, pltpu.roll(cur, 1, 1))
            beside += jnp.where(iz == nz - 1, 0.0, pltpu.roll(cur, nz - 1, 1))
            new = (1.0 - OMEGA) * cur + (sv[x] * beside + rv[x])
            dst[x] = new
            if faces:
                yst[1, 0, pl.ds(x, 1), :] = new[0:1, :]
                yst[1, 1, pl.ds(x, 1), :] = new[ny - 1 : ny, :]
            return carry

        lax.fori_loop(0, nx, slab, 0)

    wait_halo(first)
    sweep(pv, fv, 0, True)
    second = halo(1, fv)
    start_halo(second)

    per = LANES // ny

    def turn(field):
        def body(c, carry):
            part = field[pl.ds(c * per, per)].reshape(LANES, nz)
            high, low = split(jnp.transpose(part))
            ft[0:nz, at(c)] = high
            ft[nz : 2 * nz, at(c)] = low
            return carry

        lax.fori_loop(0, cells // LANES, body, 0)

    place_ids = lax.broadcasted_iota(jnp.int32, (nz, LANES), 0)
    wide = 2

    def gather(dst, scaled):
        def body(c, carry):
            off = pl.multiple_of(c * (wide * LANES), wide * LANES)
            got = jnp.dot(ft[...], hot[:, pl.ds(off, wide * LANES)], preferred_element_type=F32)
            both = got[0:nz] + got[nz : 2 * nz]
            for j in range(wide):
                r = c * wide + j
                low = jnp.bitwise_and(cell[r], nz - 1)
                part = both[:, j * LANES : (j + 1) * LANES]
                value = jnp.sum(jnp.where(place_ids == low, part, 0.0), axis=0, keepdims=True)
                if scaled:
                    value = value * pack[r, 1:2, :]
                dst[r] = value
            return carry

        lax.fori_loop(0, rows // wide, body, 0)

    loads[3].wait()
    turn(cv)
    gather(conc_at, False)

    wait_halo(second)
    sweep(fv, pv, 1, False)
    store_s = pltpu.make_async_copy(pv, out_s, store_sem.at[0])
    store_s.start()
    turn(pv)
    gather(field_at, True)
    exchange(field_at, rx1, 1)

    got_group = group.at[pl.ds(0, nf - 1)]
    pltpu.make_async_copy(got_group, got_group, group_recv).wait()
    pltpu.make_async_copy(got_group, got_group, group_send).wait()
    count = nf * tiles
    inward = tile_dir[...] == 1
    tile_hot = jnp.where(
        (lax.broadcasted_iota(jnp.int32, (tiles * kk, count), 1) == tile_links[...]) & inward, 1.0, 0.0
    ).astype(BF16)
    picked = jnp.dot(tile_hot, group[...].reshape(count, tsize), preferred_element_type=F32)
    xin[...] = picked.reshape(tiles, kk, tsize)
    xout[...] = jnp.broadcast_to(jnp.where(tile_dir[...] == 0, 1.0, 0.0), (tiles * kk, tsize)).reshape(
        tiles, kk, tsize
    )
    loads[4].wait()
    sub = lax.broadcasted_iota(jnp.int32, (2 * kk, tsize), 0)

    def flow(t, carry):
        both = jnp.concatenate([xin[t], xout[t]], axis=0).astype(BF16)
        res = lax.dot_general(both, bv[t].reshape(kk * tsize, tsize), NT, preferred_element_type=F32)
        acc = jnp.zeros((2 * kk, tsize), F32)
        for k in range(kk):
            acc += jnp.where((sub == k) | (sub == k + kk), res[:, k * tsize : (k + 1) * tsize], 0.0)
        inflow[pl.ds(t, 1), :] = jnp.sum(acc[0:kk], axis=0, keepdims=True)
        outflow[pl.ds(t, 1), :] = jnp.sum(acc[kk : 2 * kk], axis=0, keepdims=True)
        return carry

    lax.fori_loop(0, tiles, flow, 0)

    wait_exchange(rx0, 0)
    tile_ids = lax.broadcasted_iota(jnp.int32, (tiles, LANES), 0)
    frac_ids = lax.broadcasted_iota(jnp.int32, (tsize, LANES), 0)

    def prepare(r, carry):
        ids = joined(rx0[r, 0:1, :], rx0[r + rows, 0:1, :]).astype(jnp.int32)
        place[:, at(r)] = jnp.where(frac_ids == jnp.bitwise_and(ids, tsize - 1), 1.0, 0.0).astype(BF16)
        here = tile_ids == lax.shift_right_logical(ids, tbits)
        trans = joined(rx0[r, 1:2, :], rx0[r + rows, 1:2, :])
        high, low = split(jnp.where(here, trans, 0.0))
        lhs[2 * tiles : 3 * tiles, at(r)] = high
        lhs[3 * tiles : 4 * tiles, at(r)] = low
        return carry

    lax.fori_loop(0, rows, prepare, 0)

    wait_exchange(rx1, 1)

    def carried(r, carry):
        ids = joined(rx0[r, 0:1, :], rx0[r + rows, 0:1, :]).astype(jnp.int32)
        here = tile_ids == lax.shift_right_logical(ids, tbits)
        value = joined(rx1[r], rx1[r + rows])
        high, low = split(jnp.where(here, value, 0.0))
        lhs[0:tiles, at(r)] = high
        lhs[tiles : 2 * tiles, at(r)] = low
        return carry

    lax.fori_loop(0, rows, carried, 0)
    sums = lax.dot_general(lhs[...], place[...], NT, preferred_element_type=F32)
    first_sum = sums[0:tiles] + sums[tiles : 2 * tiles]
    second_sum = sums[2 * tiles : 3 * tiles] + sums[3 * tiles : 4 * tiles]
    transfer = first_sum - frac_pressure[...] * second_sum
    new_frac = frac_conc[...] + DT_FRAC * (inflow[...] - outflow[...] * frac_conc[...] + transfer)
    out_f[...] = new_frac
    high, low = split(new_frac)
    parts = jnp.concatenate([high, low], axis=0)

    def give(r, carry):
        ids = joined(rx0[r, 0:1, :], rx0[r + rows, 0:1, :]).astype(jnp.int32)
        here = tile_ids == lax.shift_right_logical(ids, tbits)
        got = jnp.dot(parts, place[:, at(r)], preferred_element_type=F32)
        rets[r] = jnp.sum(
            jnp.where(here, got[0:tiles] + got[tiles : 2 * tiles], 0.0), axis=0, keepdims=True
        )
        return carry

    lax.fori_loop(0, rows, give, 0)
    exchange(rets, rx2, 2)
    wait_exchange(rx2, 2)

    def weigh(r, carry):
        back = joined(rx2[r], rx2[r + rows])
        term = DT_MATRIX * pack[r, 1:2, :] * (back - conc_at[r])
        low_ids = jnp.bitwise_and(cell[r], nz - 1)
        high, low = split(jnp.where(place_ids == low_ids, term, 0.0))
        wt[0:nz, at(r)] = high
        wt[nz : 2 * nz, at(r)] = low
        return carry

    lax.fori_loop(0, rows, weigh, 0)
    slabs = 8

    def add(c, carry):
        size = slabs * ny
        off = pl.multiple_of(c * size, size)
        got = lax.dot_general(hot[pl.ds(off, size), :], wt[...], NT, preferred_element_type=F32)
        change = (got[:, 0:nz] + got[:, nz : 2 * nz]).reshape(slabs, ny, nz)
        where = pl.ds(c * slabs, slabs)
        cv[where] = cv[where] + change
        return carry

    lax.fori_loop(0, nx // slabs, add, 0)
    store_m = pltpu.make_async_copy(cv, out_m, store_sem.at[1])
    store_m.start()
    store_m.wait()
    store_s.wait()


def on_device(
    nm, nf,
    pressure, source, storage, matrix_conc, frac_pressure, frac_conc, tile_blocks,
    tile_links, tile_dir, link_cell, link_frac, link_trans, link_count,
):
    block = pressure.shape
    nx, ny, nz = block
    tiles, tsize = frac_conc.shape
    kk = tile_links.shape[1]
    peers, slots = link_trans.shape
    rows = peers // 2
    links = peers * slots
    live = jnp.arange(slots, dtype=jnp.int32)[None, :] < link_count[:, None]
    live_trans = jnp.where(live, link_trans, 0.0)

    def paired(a):
        return jnp.concatenate([a[:rows], a[rows:]], axis=1)

    cell = paired(link_cell)[:, None, :]
    pack = jnp.stack([paired(link_frac).astype(F32), paired(live_trans)], axis=1)
    hbm = pl.BlockSpec(memory_space=pl.ANY)
    vmem = pl.BlockSpec(memory_space=pltpu.VMEM)
    field = pltpu.VMEM(block, F32)
    row = pltpu.VMEM((rows, 1, LANES), F32)
    dma = pltpu.SemaphoreType.DMA
    return pl.pallas_call(
        functools.partial(kernel, nm, nf),
        out_shape=(
            jax.ShapeDtypeStruct(block, F32),
            jax.ShapeDtypeStruct(block, F32),
            jax.ShapeDtypeStruct((tiles, tsize), F32),
        ),
        in_specs=[hbm] * 5 + [vmem] * 6,
        out_specs=(hbm, hbm, vmem),
        scratch_shapes=[
            field, field, field, field, field,
            pltpu.VMEM(tile_blocks.shape, BF16),
            pltpu.VMEM((2, 2, nx, nz), F32),
            pltpu.VMEM((2, 2, ny, nz), F32),
            pltpu.VMEM((2, 2, nx, nz), F32),
            pltpu.VMEM((nx * ny, links), BF16),
            pltpu.VMEM((2 * nz, nx * ny), BF16),
            pltpu.VMEM((tsize, links), BF16),
            pltpu.VMEM((4 * tiles, links), BF16),
            pltpu.VMEM((2 * nz, links), BF16),
            row, row, row,
            pltpu.VMEM((peers, 2, LANES), F32),
            pltpu.VMEM((peers, 1, LANES), F32),
            pltpu.VMEM((peers, 1, LANES), F32),
            pltpu.VMEM((nf, tiles, tsize), BF16),
            pltpu.VMEM((tiles, kk, tsize), F32),
            pltpu.VMEM((tiles, kk, tsize), F32),
            pltpu.VMEM((tiles, tsize), F32),
            pltpu.VMEM((tiles, tsize), F32),
            dma((5,)), dma((2,)), dma((2, 4)), dma((2, 4)), dma((3,)), dma((3,)), dma, dma,
        ],
        compiler_params=pltpu.CompilerParams(
            collective_id=0, has_side_effects=True, vmem_limit_bytes=56 * 1024 * 1024
        ),
    )(
        pressure, source, storage, matrix_conc, tile_blocks, frac_pressure, frac_conc,
        tile_links.reshape(-1, 1), tile_dir.reshape(-1, 1), cell, pack,
    )


def solution(mesh):
    grid = P("mat", "frac", None)
    own = P(("mat", "frac"), None)
    in_specs = (
        grid, grid, grid, grid, own, own, P(("mat", "frac"), None, None, None),
        own, own, own, own, own, P(("mat", "frac")),
    )
    return jax.shard_map(
        functools.partial(on_device, mesh.shape["mat"], mesh.shape["frac"]),
        mesh=mesh, in_specs=in_specs, out_specs=(grid, grid, own), check_vma=False,
    )
```

```python
import functools

import jax
import jax.numpy as jnp
from jax import lax
from jax.experimental import pallas as pl
from jax.experimental.pallas import tpu as pltpu
from jax.sharding import PartitionSpec as P

OMEGA = 0.8
DT_FRAC = 0.1
DT_MATRIX = 0.5
MESH = pl.DeviceIdType.MESH
F32 = jnp.float32
BF16 = jnp.bfloat16
LANES = 128
NT = (((1,), (1,)), ((), ()))


def split(v):
    high = v.astype(BF16)
    return high, (v - high.astype(F32)).astype(BF16)


def kernel(
    nm, nf,
    pressure, source, storage, conc, blocks, frac_pressure, frac_conc, tile_links, tile_dir, link_cell, link_frac, link_trans, link_count,
    out_s, out_m, out_f,
    pv, sv, rv, cv, fv, bv, cell, frac_rows, trans_rows, pack, tile_hot, yst, hx, hy, hot, ft, place, lhs, wt,
    conc_at, field_at, rets, rx0, rx1, rx2, group, xin, xout, inflow, outflow,
    load_sem, store_sem, halo_send, halo_recv, a2a_send, a2a_recv, group_send, group_recv,
):
    m, f = lax.axis_index("mat"), lax.axis_index("frac")
    peers = nm * nf
    rows = peers // 2
    me = m * nf + f
    nx, ny, nz = pv.shape
    zbits = nz.bit_length() - 1
    tiles, tsize = frac_conc.shape
    tbits = tsize.bit_length() - 1
    kk = bv.shape[1]
    cells = nx * ny

    loads = [
        pltpu.make_async_copy(a, b, load_sem.at[i])
        for i, (a, b) in enumerate(
            ((pressure, pv), (storage, sv), (source, rv), (conc, cv), (blocks, bv))
        )
    ]
    for copy in loads:
        copy.start()

    barrier = pltpu.get_barrier_semaphore()

    def greet(i, carry):
        dest = lax.rem(me + i, peers)
        pl.semaphore_signal(
            barrier, inc=1, device_id=(lax.div(dest, nf), lax.rem(dest, nf)), device_id_type=MESH
        )
        return carry

    lax.fori_loop(1, peers, greet, 0)

    @pl.when(m == 0)
    def _():
        for k in range(2):
            hx[k, 0] = jnp.zeros((ny, nz), F32)

    @pl.when(m == nm - 1)
    def _():
        for k in range(2):
            hx[k, 1] = jnp.zeros((ny, nz), F32)

    @pl.when(f == 0)
    def _():
        for k in range(2):
            hy[k, 0] = jnp.zeros((nx, nz), F32)

    @pl.when(f == nf - 1)
    def _():
        for k in range(2):
            hy[k, 1] = jnp.zeros((nx, nz), F32)

    group[f] = frac_conc[...].astype(BF16)
    lane = lax.broadcasted_iota(jnp.int32, (1, LANES), 1)
    slots = LANES // 2
    left = lane < slots

    def paired(ref):
        return jnp.concatenate([ref[0:rows, :], ref[rows : 2 * rows, :]], axis=1)

    cell[...] = paired(link_cell)
    frac_rows[...] = paired(link_frac).astype(F32)
    trans_rows[...] = paired(link_trans)

    def fill(r, carry):
        bound = jnp.where(left, link_count[r], link_count[r + rows] + slots)
        pack[r, 0:1, :] = frac_rows[pl.ds(r, 1), :]
        pack[r, 1:2, :] = jnp.where(lane < bound, trans_rows[pl.ds(r, 1), :], 0.0)
        return carry

    lax.fori_loop(0, rows, fill, 0)

    loads[0].wait()

    def stage(x, carry):
        yst[0, 0, pl.ds(x, 1), :] = pv[x, 0:1, :]
        yst[0, 1, pl.ds(x, 1), :] = pv[x, ny - 1 : ny, :]
        return carry

    lax.fori_loop(0, nx, stage, 0)

    def halo(k, field):
        out = []
        for d, (src, dst, to, sends, gets) in enumerate((
            (field.at[0], hx.at[k, 1], (m - 1, f), m > 0, m < nm - 1),
            (field.at[nx - 1], hx.at[k, 0], (m + 1, f), m < nm - 1, m > 0),
            (yst.at[k, 0], hy.at[k, 1], (m, f - 1), f > 0, f < nf - 1),
            (yst.at[k, 1], hy.at[k, 0], (m, f + 1), f < nf - 1, f > 0),
        )):
            copy = pltpu.make_async_remote_copy(
                src_ref=src, dst_ref=dst, send_sem=halo_send.at[k, d], recv_sem=halo_recv.at[k, d],
                device_id=to, device_id_type=MESH,
            )
            out.append((copy, sends, gets))
        return out

    def start_halo(copies):
        for copy, sends, gets in copies:
            pl.when(sends)(copy.start)

    def wait_halo(copies):
        for copy, sends, gets in copies:
            pl.when(gets)(copy.wait_recv)
        for copy, sends, gets in copies:
            pl.when(sends)(copy.wait_send)

    def exchange(src, dst, k):
        def send(i, carry):
            dest = lax.rem(me + i, peers)
            pltpu.make_async_remote_copy(
                src_ref=src.at[lax.rem(dest, rows)], dst_ref=dst.at[me],
                send_sem=a2a_send.at[k], recv_sem=a2a_recv.at[k],
                device_id=(lax.div(dest, nf), lax.rem(dest, nf)), device_id_type=MESH,
            ).start()
            return carry

        lax.fori_loop(1, peers, send, 0)
        dst[me] = src[lax.rem(me, rows)]

    def wait_exchange(dst, k):
        part = dst.at[pl.ds(0, peers - 1)]
        pltpu.make_async_copy(part, part, a2a_recv.at[k]).wait()
        pltpu.make_async_copy(part, part, a2a_send.at[k]).wait()

    pl.semaphore_wait(barrier, peers - 1)
    first = halo(0, pv)
    start_halo(first)
    exchange(pack, rx0, 0)

    def spread(i, carry):
        pltpu.make_async_remote_copy(
            src_ref=group.at[f], dst_ref=group.at[f], send_sem=group_send, recv_sem=group_recv,
            device_id=(m, lax.rem(f + i, nf)), device_id_type=MESH,
        ).start()
        return carry

    lax.fori_loop(1, nf, spread, 0)

    upper = me >= rows

    def joined(a, b):
        a = jnp.where(upper, pltpu.roll(a, LANES // 2, 1), a)
        b = jnp.where(upper, b, pltpu.roll(b, LANES // 2, 1))
        return jnp.where(left, a, b)

    def at(r):
        return pl.ds(pl.multiple_of(r * LANES, LANES), LANES)

    row_ids = lax.broadcasted_iota(jnp.int32, (cells, LANES), 0)

    def mark(r, carry):
        high = lax.shift_right_logical(cell[pl.ds(r, 1), :], zbits)
        hot[:, at(r)] = jnp.where(row_ids == high, 1.0, 0.0).astype(BF16)
        return carry

    lax.fori_loop(0, rows, mark, 0)

    loads[1].wait()
    loads[2].wait()

    def factors(x, carry):
        scale = OMEGA / (6.0 + sv[x])
        sv[x] = scale
        rv[x] = rv[x] * scale
        return carry

    lax.fori_loop(0, nx, factors, 0)

    iy = lax.broadcasted_iota(jnp.int32, (ny, nz), 0)
    iz = lax.broadcasted_iota(jnp.int32, (ny, nz), 1)

    def sweep(src, dst, k, faces):
        def slab(x, carry):
            cur = src[x]
            before = jnp.where(x == 0, hx[k, 0], src[jnp.maximum(x - 1, 0)])
            after = jnp.where(x == nx - 1, hx[k, 1], src[jnp.minimum(x + 1, nx - 1)])
            beside = before + after
            beside += jnp.where(iy == 0, hy[k, 0, pl.ds(x, 1), :], pltpu.roll(cur, 1, 0))
            beside += jnp.where(iy == ny - 1, hy[k, 1, pl.ds(x, 1), :], pltpu.roll(cur, ny - 1, 0))
            beside += jnp.where(iz == 0, 0.0, pltpu.roll(cur, 1, 1))
            beside += jnp.where(iz == nz - 1, 0.0, pltpu.roll(cur, nz - 1, 1))
            new = (1.0 - OMEGA) * cur + (sv[x] * beside + rv[x])
            dst[x] = new
            if faces:
                yst[1, 0, pl.ds(x, 1), :] = new[0:1, :]
                yst[1, 1, pl.ds(x, 1), :] = new[ny - 1 : ny, :]
            return carry

        lax.fori_loop(0, nx, slab, 0, unroll=2)

    wait_halo(first)
    sweep(pv, fv, 0, True)
    second = halo(1, fv)
    start_halo(second)

    per = LANES // ny

    def turn(field):
        def body(c, carry):
            part = field[pl.ds(c * per, per)].reshape(LANES, nz)
            high, low = split(jnp.transpose(part))
            ft[0:nz, at(c)] = high
            ft[nz : 2 * nz, at(c)] = low
            return carry

        lax.fori_loop(0, cells // LANES, body, 0)

    place_ids = lax.broadcasted_iota(jnp.int32, (nz, LANES), 0)
    wide = 2

    def gather(dst, scaled):
        def body(c, carry):
            off = pl.multiple_of(c * (wide * LANES), wide * LANES)
            got = jnp.dot(ft[...], hot[:, pl.ds(off, wide * LANES)], preferred_element_type=F32)
            both = got[0:nz] + got[nz : 2 * nz]
            for j in range(wide):
                r = c * wide + j
                low = jnp.bitwise_and(cell[pl.ds(r, 1), :], nz - 1)
                part = both[:, j * LANES : (j + 1) * LANES]
                value = jnp.sum(jnp.where(place_ids == low, part, 0.0), axis=0, keepdims=True)
                if scaled:
                    value = value * pack[r, 1:2, :]
                dst[r] = value
            return carry

        lax.fori_loop(0, rows // wide, body, 0)

    loads[3].wait()
    turn(cv)
    gather(conc_at, False)

    wait_halo(second)
    sweep(fv, pv, 1, False)
    store_s = pltpu.make_async_copy(pv, out_s, store_sem.at[0])
    store_s.start()
    turn(pv)
    gather(field_at, True)
    exchange(field_at, rx1, 1)

    got_group = group.at[pl.ds(0, nf - 1)]
    pltpu.make_async_copy(got_group, got_group, group_recv).wait()
    pltpu.make_async_copy(got_group, got_group, group_send).wait()
    count = nf * tiles
    tile_no = lax.broadcasted_iota(jnp.int32, (kk, count), 1)
    for t in range(tiles):
        inward = tile_dir[:, t : t + 1] == 1
        chosen = (tile_no == tile_links[:, t : t + 1]) & inward
        tile_hot[t * kk : (t + 1) * kk, :] = jnp.where(chosen, 1.0, 0.0)
        xout[t] = jnp.broadcast_to(jnp.where(inward, 0.0, 1.0), (kk, tsize))
    picked = jnp.dot(
        tile_hot[...].astype(BF16), group[...].reshape(count, tsize), preferred_element_type=F32
    )
    xin[...] = picked.reshape(tiles, kk, tsize)
    loads[4].wait()
    sub = lax.broadcasted_iota(jnp.int32, (2 * kk, tsize), 0)

    def flow(t, carry):
        both = jnp.concatenate([xin[t], xout[t]], axis=0).astype(BF16)
        res = lax.dot_general(both, bv[t].reshape(kk * tsize, tsize), NT, preferred_element_type=F32)
        acc = jnp.zeros((2 * kk, tsize), F32)
        for k in range(kk):
            acc += jnp.where((sub == k) | (sub == k + kk), res[:, k * tsize : (k + 1) * tsize], 0.0)
        inflow[pl.ds(t, 1), :] = jnp.sum(acc[0:kk], axis=0, keepdims=True)
        outflow[pl.ds(t, 1), :] = jnp.sum(acc[kk : 2 * kk], axis=0, keepdims=True)
        return carry

    lax.fori_loop(0, tiles, flow, 0)

    wait_exchange(rx0, 0)
    tile_ids = lax.broadcasted_iota(jnp.int32, (tiles, LANES), 0)
    frac_ids = lax.broadcasted_iota(jnp.int32, (tsize, LANES), 0)

    def prepare(r, carry):
        ids = joined(rx0[r, 0:1, :], rx0[r + rows, 0:1, :]).astype(jnp.int32)
        place[:, at(r)] = jnp.where(frac_ids == jnp.bitwise_and(ids, tsize - 1), 1.0, 0.0).astype(BF16)
        here = tile_ids == lax.shift_right_logical(ids, tbits)
        trans = joined(rx0[r, 1:2, :], rx0[r + rows, 1:2, :])
        high, low = split(jnp.where(here, trans, 0.0))
        lhs[2 * tiles : 3 * tiles, at(r)] = high
        lhs[3 * tiles : 4 * tiles, at(r)] = low
        return carry

    lax.fori_loop(0, rows, prepare, 0, unroll=4)

    wait_exchange(rx1, 1)

    def carried(r, carry):
        ids = joined(rx0[r, 0:1, :], rx0[r + rows, 0:1, :]).astype(jnp.int32)
        here = tile_ids == lax.shift_right_logical(ids, tbits)
        value = joined(rx1[r], rx1[r + rows])
        high, low = split(jnp.where(here, value, 0.0))
        lhs[0:tiles, at(r)] = high
        lhs[tiles : 2 * tiles, at(r)] = low
        return carry

    lax.fori_loop(0, rows, carried, 0, unroll=4)
    sums = lax.dot_general(lhs[...], place[...], NT, preferred_element_type=F32)
    first_sum = sums[0:tiles] + sums[tiles : 2 * tiles]
    second_sum = sums[2 * tiles : 3 * tiles] + sums[3 * tiles : 4 * tiles]
    transfer = first_sum - frac_pressure[...] * second_sum
    new_frac = frac_conc[...] + DT_FRAC * (inflow[...] - outflow[...] * frac_conc[...] + transfer)
    out_f[...] = new_frac
    high, low = split(new_frac)
    parts = jnp.concatenate([high, low], axis=0)

    def give(r, carry):
        ids = joined(rx0[r, 0:1, :], rx0[r + rows, 0:1, :]).astype(jnp.int32)
        here = tile_ids == lax.shift_right_logical(ids, tbits)
        got = jnp.dot(parts, place[:, at(r)], preferred_element_type=F32)
        rets[r] = jnp.sum(
            jnp.where(here, got[0:tiles] + got[tiles : 2 * tiles], 0.0), axis=0, keepdims=True
        )
        return carry

    lax.fori_loop(0, rows, give, 0, unroll=4)
    exchange(rets, rx2, 2)
    wait_exchange(rx2, 2)

    def weigh(r, carry):
        back = joined(rx2[r], rx2[r + rows])
        term = DT_MATRIX * pack[r, 1:2, :] * (back - conc_at[r])
        low_ids = jnp.bitwise_and(cell[pl.ds(r, 1), :], nz - 1)
        high, low = split(jnp.where(place_ids == low_ids, term, 0.0))
        wt[0:nz, at(r)] = high
        wt[nz : 2 * nz, at(r)] = low
        return carry

    lax.fori_loop(0, rows, weigh, 0, unroll=2)
    slabs = 8

    def add(c, carry):
        size = slabs * ny
        off = pl.multiple_of(c * size, size)
        got = lax.dot_general(hot[pl.ds(off, size), :], wt[...], NT, preferred_element_type=F32)
        change = (got[:, 0:nz] + got[:, nz : 2 * nz]).reshape(slabs, ny, nz)
        where = pl.ds(c * slabs, slabs)
        cv[where] = cv[where] + change
        return carry

    lax.fori_loop(0, nx // slabs, add, 0)
    store_m = pltpu.make_async_copy(cv, out_m, store_sem.at[1])
    store_m.start()
    store_m.wait()
    store_s.wait()


def on_device(
    nm, nf,
    pressure, source, storage, matrix_conc, frac_pressure, frac_conc, tile_blocks,
    tile_links, tile_dir, link_cell, link_frac, link_trans, link_count,
):
    block = pressure.shape
    nx, ny, nz = block
    tiles, tsize = frac_conc.shape
    kk = tile_links.shape[1]
    peers, slots = link_trans.shape
    rows = peers // 2
    links = peers * slots
    hbm = pl.BlockSpec(memory_space=pltpu.HBM)
    free = pl.BlockSpec(memory_space=pl.ANY)
    vmem = pl.BlockSpec(memory_space=pltpu.VMEM)
    smem = pl.BlockSpec(memory_space=pltpu.SMEM)
    field = pltpu.VMEM(block, F32)
    row = pltpu.VMEM((rows, 1, LANES), F32)
    dma = pltpu.SemaphoreType.DMA
    return pl.pallas_call(
        functools.partial(kernel, nm, nf),
        out_shape=(
            jax.ShapeDtypeStruct(block, F32),
            jax.ShapeDtypeStruct(block, F32),
            jax.ShapeDtypeStruct((tiles, tsize), F32),
        ),
        in_specs=[hbm] * 5 + [vmem] * 7 + [smem],
        out_specs=(free, free, vmem),
        scratch_shapes=[
            field, field, field, field, field,
            pltpu.VMEM(tile_blocks.shape, BF16),
            pltpu.VMEM((rows, LANES), jnp.int32),
            pltpu.VMEM((rows, LANES), F32),
            pltpu.VMEM((rows, LANES), F32),
            pltpu.VMEM((rows, 2, LANES), F32),
            pltpu.VMEM((tiles * kk, nf * tiles), F32),
            pltpu.VMEM((2, 2, nx, nz), F32),
            pltpu.VMEM((2, 2, ny, nz), F32),
            pltpu.VMEM((2, 2, nx, nz), F32),
            pltpu.VMEM((nx * ny, links), BF16),
            pltpu.VMEM((2 * nz, nx * ny), BF16),
            pltpu.VMEM((tsize, links), BF16),
            pltpu.VMEM((4 * tiles, links), BF16),
            pltpu.VMEM((2 * nz, links), BF16),
            row, row, row,
            pltpu.VMEM((peers, 2, LANES), F32),
            pltpu.VMEM((peers, 1, LANES), F32),
            pltpu.VMEM((peers, 1, LANES), F32),
            pltpu.VMEM((nf, tiles, tsize), BF16),
            pltpu.VMEM((tiles, kk, tsize), F32),
            pltpu.VMEM((tiles, kk, tsize), F32),
            pltpu.VMEM((tiles, tsize), F32),
            pltpu.VMEM((tiles, tsize), F32),
            dma((5,)), dma((2,)), dma((2, 4)), dma((2, 4)), dma((3,)), dma((3,)), dma, dma,
        ],
        compiler_params=pltpu.CompilerParams(
            collective_id=0, has_side_effects=True, vmem_limit_bytes=56 * 1024 * 1024
        ),
    )(
        pressure, source, storage, matrix_conc, tile_blocks, frac_pressure, frac_conc,
        tile_links.T, tile_dir.T, link_cell, link_frac, link_trans, link_count,
    )


def solution(mesh):
    grid = P("mat", "frac", None)
    own = P(("mat", "frac"), None)
    in_specs = (
        grid, grid, grid, grid, own, own, P(("mat", "frac"), None, None, None),
        own, own, own, own, own, P(("mat", "frac")),
    )
    return jax.shard_map(
        functools.partial(on_device, mesh.shape["mat"], mesh.shape["frac"]),
        mesh=mesh, in_specs=in_specs, out_specs=(grid, grid, own), check_vma=False,
    )
```
